256 devices in a mesh: wide: 32 (over z, x), narrow: 8 (over y, core).
Axes of the slice: x: 4, y: 4, z: 8, core: 2. Of those that a mesh axis runs over, the one named last changes fastest.
Arguments:
- integrals: bfloat16 [32, 64, 64, 8192], P('wide', None, None, 'narrow'), may hold values from -6 to 6
- occupied_coeffs: bfloat16 [4, 20480], P(None, 'wide'), may hold values from -0.75 to 0.75
- metric: bfloat16 [8192, 8192], P('narrow', 'wide'), may hold values from -0.125 to 0.125
- mu_block: int32 [32], P('wide'), may hold values from 0 to 319
- pair_count: int32 [32], P('wide'), may hold values from 8 to 64
- destination: int32 [1024], P('wide'), may hold values from 0 to 31, as said below
Outputs:
- placed: bfloat16 [2048, 8, 8192], P('wide', None, 'narrow')
The draws below stay inside these ranges and needn't reach their ends.
Inputs may be any that keep to these rules, and one draw needn't show every extreme that they name: Among the 32 items of one wide device at most 2 name the same destination; in every draw one destination receives exactly 2 items from every wide device.
All inputs are finite; a program needn't handle non-finite values.
Results may differ from the reference program's by a relative error of at most 0.017.
Values may be sent and summed in bfloat16 or wider, within the bound.
No kernel may reach another device: no remote copies, remote signals or barrier semaphores. Data moves between devices by JAX's collectives and lax.ppermute only.
A program may use at most 128 MiB of HBM per device.

```python
import jax
import jax.numpy as jnp
from jax import lax

NAO = 20480
AUX = 8192
BW = 64
NU = 64
GROUP = 2
OB = 4
NBLK = 32
NAOB = 320
ITEMS_DEV = 32
NITEMS = 1024
SOURCES = 32
CAP = 2
SLOTS = 64
N_NARROW = 8


def draw_destination(key, part):
    key = jax.random.fold_in(key, 7)
    busiest = jax.random.randint(jax.random.fold_in(key, 1), (), 0, SOURCES).astype(jnp.int32)

    def one_source(source):
        source_key = jax.random.fold_in(key, source + 11)
        other_slots = jax.random.permutation(jax.random.fold_in(source_key, 1), (SOURCES - 1) * CAP)[:ITEMS_DEV - CAP]
        other_dest = (other_slots // CAP).astype(jnp.int32)
        other_dest = other_dest + (other_dest >= busiest).astype(jnp.int32)
        all_dest = jnp.concatenate([jnp.full((CAP,), 0, jnp.int32) + busiest, other_dest])
        shuffle = jax.random.permutation(jax.random.fold_in(source_key, 2), ITEMS_DEV)
        return all_dest[shuffle]
    return jax.vmap(one_source)(jnp.arange(SOURCES, dtype=jnp.int32)).reshape(-1).astype(jnp.int32)


def with_ends(result, stream_key, least, largest):
    spot = [jax.random.randint(jax.random.fold_in(stream_key, axis), (), 0, length) for axis, length in enumerate(result.shape)]
    main_axis = result.shape.index(max(result.shape))
    beside = spot[:main_axis] + [(spot[main_axis] + 1) % result.shape[main_axis]] + spot[main_axis + 1:]
    return result.at[tuple(spot)].set(least).at[tuple(beside)].set(largest)


def raised(array, own_key, source, target, parts, factor):
    def block_of(axis_at):
        return (jnp.arange(array.shape[axis_at]) // (array.shape[axis_at] // parts)).reshape((-1,) + (1,) * (array.ndim - 1 - axis_at))

    near = jax.random.permutation(own_key, parts)[block_of(target)]
    second = (block_of(target) + parts // 2) % parts
    return jnp.where((block_of(source) == near) | (block_of(source) == second), factor * array, array)


def levels(key, shape, shards, low, high):
    gain = 1.0
    for axis_at, blocks in shards:
        steps = jax.random.uniform(jax.random.fold_in(jax.random.fold_in(key, 6), axis_at), (blocks,), jnp.float32, low / len(shards), high / len(shards))
        gain = gain * jnp.repeat(jnp.exp(steps), shape[axis_at] // blocks).reshape((-1,) + (1,) * (len(shape) - 1 - axis_at))
    return gain


def gaussian(rng, extent, scale, limit, split=(), kind=jnp.bfloat16):
    entries = scale * jax.random.normal(rng, extent, jnp.float32)
    if split:
        entries = entries * levels(rng, extent, split, -0.22, 0.18)
    return jnp.clip(entries, -limit, limit).astype(kind)


def noise_with(own_key, dims, scale, bound, shards, heavy, kind=jnp.bfloat16):
    result = scale * jax.random.normal(own_key, dims, jnp.float32)
    if shards:
        result = result * levels(own_key, dims, shards, -0.22, 0.18)
    return jnp.clip(raised(result, jax.random.fold_in(own_key, 3), *heavy), -bound, bound).astype(kind)


def setup_inputs(seed: int = 0) -> dict:
    splits = jax.random.split(jax.random.key(seed), 7)
    return {
        "integrals": gaussian(splits[0], (NBLK, BW, NU, AUX), 1.0, 6.0, ((0, 32), (3, 8))),
        "occupied_coeffs": gaussian(splits[1], (OB, NAO), BW ** -0.5, 0.75, ((1, 32),)),
        "metric": noise_with(splits[2], (AUX, AUX), AUX ** -0.5, 0.125, ((0, 8), (1, 32)), (0, 1, 32, 2.75)),
        "mu_block": with_ends(jax.random.randint(splits[3], (NBLK,), 0, NAOB), jax.random.fold_in(splits[3], 1), 0, NAOB - 1).astype(jnp.int32),
        "pair_count": with_ends(jax.random.randint(splits[4], (NBLK,), NU // 8, NU + 1), jax.random.fold_in(splits[4], 1), NU // 8, NU).astype(jnp.int32),
        "destination": draw_destination(jax.random.fold_in(splits[6], 71), 0),
    }


def transform_block(block_tile, occupied_coeffs, first_block, live_count):
    coeff_block = lax.dynamic_slice_in_dim(occupied_coeffs, (first_block * BW).astype(jnp.int32), BW, 1)
    keep_mask = (jnp.arange(NU, dtype=jnp.int32) < live_count)[None, :, None]
    block_tile = jnp.where(keep_mask, block_tile, jnp.zeros_like(block_tile))
    return jnp.einsum("im,mnp->nip", coeff_block.astype(jnp.float32), block_tile.astype(jnp.float32)).astype(jnp.bfloat16)


def metric_block(halves, metric_slabs):
    row_data = halves.reshape(NU * OB, N_NARROW, AUX // N_NARROW).astype(jnp.float32)
    partial_value = jnp.einsum("rnp,npq->nrq", row_data, metric_slabs).astype(jnp.bfloat16)
    partial_value = lax.optimization_barrier(partial_value)
    return jnp.sum(partial_value.astype(jnp.float32), axis=0).astype(jnp.bfloat16)


def reference(integrals, occupied_coeffs, metric, mu_block, pair_count, destination):
    metric_slabs = metric.reshape(N_NARROW, AUX // N_NARROW, AUX).astype(jnp.float32)

    def block_result(packed):
        block_tile, first_block, live_count = packed
        halves = transform_block(block_tile, occupied_coeffs, first_block, live_count)
        return metric_block(halves, metric_slabs).reshape(NU // GROUP, GROUP * OB, AUX)

    results = lax.map(block_result, (integrals, mu_block, pair_count))
    results = results.reshape(NITEMS, GROUP * OB, AUX)
    dest_grid = destination.reshape(SOURCES, ITEMS_DEV)
    same_dest = dest_grid[:, :, None] == dest_grid[:, None, :]
    earlier = jnp.arange(ITEMS_DEV)[:, None] > jnp.arange(ITEMS_DEV)[None, :]
    slot_rank = jnp.sum((same_dest & earlier[None]).astype(jnp.int32), axis=2)
    target = dest_grid * SLOTS + jnp.arange(SOURCES, dtype=jnp.int32)[:, None] * CAP + slot_rank
    placed = jnp.zeros((SOURCES * SLOTS, GROUP * OB, AUX), jnp.bfloat16)
    return placed.at[target.reshape(-1).astype(jnp.int32)].set(results)
```

```python
import jax
import jax.numpy as jnp
from jax import lax
from jax.sharding import Mesh, PartitionSpec as P


def small_gather(occupied_coeffs, destination):
    rows = occupied_coeffs.shape[0]
    packed = jnp.concatenate(
        [occupied_coeffs, destination.astype(jnp.bfloat16).reshape(rows, -1)], axis=1
    )
    gathered = lax.all_gather(packed, ("z", "x"), axis=0)
    width = occupied_coeffs.shape[1]
    coeffs = gathered[:, :, :width]
    dests = gathered[:, :, width:].reshape(gathered.shape[0], -1).astype(jnp.int32)
    return coeffs, dests


def half_transform(block, coeff_block, live_count):
    mu, nu, p = block.shape
    i = coeff_block.shape[0]
    ids = jnp.arange(nu, dtype=jnp.int32)
    same = (ids[:, None] == ids[None, :]) & (ids[:, None] < live_count)
    weights = jnp.where(
        same[:, None, None, :], coeff_block[None, :, :, None], jnp.zeros((), jnp.bfloat16)
    ).reshape(nu * i, mu * nu)
    return jnp.dot(
        weights, block.reshape(mu * nu, p), preferred_element_type=jnp.float32
    ).astype(jnp.bfloat16)


def per_device(integrals, occupied_coeffs, metric, mu_block, pair_count, destination):
    nz, nx = lax.axis_size("z"), lax.axis_size("x")
    peers = nz * nx
    item_count = destination.shape[0]
    cap = max(2, (2 * item_count + peers - 1) // peers)
    _, mu_width, nu, p_local = integrals.shape
    orbitals = occupied_coeffs.shape[0]
    item_rows = nu * orbitals // item_count

    metric_z = lax.all_gather(metric, "z", axis=0)
    coeffs, dests = small_gather(occupied_coeffs, destination)
    blocks_per = occupied_coeffs.shape[1] // mu_width
    first = mu_block[0]
    coeff_block = lax.dynamic_slice(
        coeffs, (first // blocks_per, 0, (first % blocks_per) * mu_width), (1, orbitals, mu_width)
    )[0]
    halves = half_transform(integrals[0], coeff_block, pair_count[0])
    items = lax.all_gather(halves, "x", axis=0, tiled=True)
    partial = jnp.einsum("rp,zpq->zrq", items, metric_z, preferred_element_type=jnp.float32).astype(
        jnp.bfloat16
    )
    summed = lax.psum_scatter(partial, ("y", "core"), scatter_dimension=0, tiled=False)
    q = summed.shape[-1]

    my_dests = lax.dynamic_slice_in_dim(dests, lax.axis_index("z") * nx, nx, 0)
    same = my_dests[:, :, None] == my_dests[:, None, :]
    ids = jnp.arange(item_count)
    rank = jnp.sum((same & (ids[:, None] > ids[None, :])).astype(jnp.int32), axis=2)
    target = my_dests * cap + rank
    placing = (
        target[:, None, :] == jnp.arange(peers * cap, dtype=jnp.int32)[None, :, None]
    ).astype(jnp.bfloat16)
    outgoing = jnp.einsum(
        "xsj,xjc->sxc",
        placing,
        summed.reshape(nx, item_count, item_rows * q),
        preferred_element_type=jnp.float32,
    ).astype(jnp.bfloat16)
    outgoing = outgoing.reshape(peers, cap, nx, item_rows, q)
    arrived = lax.all_to_all(outgoing, ("z", "x"), split_axis=0, concat_axis=0, tiled=True)
    arrived = arrived.reshape(nz, nx, cap, nx, item_rows, q).transpose(0, 3, 2, 4, 1, 5)
    return arrived.reshape(peers * cap, item_rows, nx * q)


def solution(mesh):
    n_narrow = mesh.shape["narrow"]
    grid = mesh.devices.reshape(8, 4, n_narrow // 2, 2)
    fine = Mesh(grid, ("z", "x", "y", "core"))
    wide, narrow = ("z", "x"), ("y", "core")
    placed = (
        P(wide, None, None, narrow),
        P(None, wide),
        P(narrow, wide),
        P(wide),
        P(wide),
        P(wide),
    )
    return jax.shard_map(
        per_device, mesh=fine, in_specs=placed, out_specs=P(wide, None, narrow), check_vma=False
    )
```

```python
import functools

import jax
import jax.numpy as jnp
from jax import lax
from jax.experimental import pallas as pl
from jax.experimental.pallas import tpu as pltpu
from jax.sharding import Mesh, PartitionSpec as P

BF = jnp.bfloat16
F32 = jnp.float32
VMEM_LIMIT = 48 * 1024 * 1024


def shift(size, step):
    return [(i, (i + step) % size) for i in range(size)]


def params():
    return pltpu.CompilerParams(vmem_limit_bytes=VMEM_LIMIT)


def halves_kernel(where, packed_ref, block_ref, out_ref, weight, *, nu, orbitals):
    width, group, p = block_ref.shape
    rows, depth = group * orbitals, width * group
    lanes, packs = packed_ref.shape[2], packed_ref.shape[1]

    def iota(shape, dim):
        return lax.broadcasted_iota(jnp.int32, shape, dim)

    def dot(left, right):
        return jnp.dot(left, right, preferred_element_type=F32)

    pick = iota((lanes, width), 0) == where[1] * width + iota((lanes, width), 1)
    chosen = dot(packed_ref[0], pick.astype(BF)).astype(BF)
    repeat = lax.rem(iota((rows, packs), 0), orbitals) == iota((rows, packs), 1)
    coeff = dot(repeat.astype(BF), chosen).astype(BF)
    spread = iota((width, depth), 0) == iota((width, depth), 1) // group
    wide = dot(coeff, spread.astype(BF))
    row_nu = iota((rows, depth), 0) // orbitals
    col_nu = lax.rem(iota((rows, depth), 1), group)
    live = pl.program_id(0) * group + row_nu < where[2]
    weight[...] = jnp.where((row_nu == col_nu) & live, wide, 0.0).astype(BF)
    out_ref[...] = dot(weight[...], block_ref[...].reshape(depth, p)).astype(BF)


def half_transform(where, packed, block, orbitals):
    mu, nu, p = block.shape
    group = 32
    rows = group * orbitals
    return pl.pallas_call(
        functools.partial(halves_kernel, nu=nu, orbitals=orbitals),
        grid_spec=pltpu.PrefetchScalarGridSpec(
            num_scalar_prefetch=1,
            grid=(nu // group,),
            in_specs=[
                pl.BlockSpec((1,) + packed.shape[1:], lambda s, w: (w[0], 0, 0)),
                pl.BlockSpec((mu, group, p), lambda s, w: (0, s, 0)),
            ],
            out_specs=pl.BlockSpec((rows, p), lambda s, w: (s, 0)),
            scratch_shapes=[pltpu.VMEM((rows, mu * group), BF)],
        ),
        out_shape=jax.ShapeDtypeStruct((nu * orbitals, p), BF),
        compiler_params=params(),
        cost_estimate=pl.CostEstimate(
            flops=2 * rows * mu * nu * p, bytes_accessed=2 * mu * nu * p, transcendentals=0
        ),
        name="halves",
    )(where, packed, block)


def product_kernel(order, *refs, items, pieces, steps, with_arrived):
    refs = list(refs)
    rows = [refs.pop(0) for _ in range(items)]
    blocks = [[refs.pop(0) for _ in range(n)] for n in pieces]
    arrived = [refs.pop(0) for _ in range(steps)] if with_arrived else None
    outs = [refs.pop(0) for _ in range(steps)]
    held, sems = refs

    def copies(step, block):
        at = 0
        for part, ref in enumerate(block):
            depth = ref.shape[0]
            yield pltpu.make_async_copy(ref, held.at[step, pl.ds(at, depth)], sems.at[step, part])
            at += depth

    for step in range(steps):
        for d, block in enumerate(blocks):

            @pl.when(order[step] == d)
            def _(step=step, block=block):
                for copy in copies(step, block):
                    copy.start()

    for step in range(steps):
        for d, block in enumerate(blocks):

            @pl.when(order[step] == d)
            def _(step=step, block=block):
                for copy in copies(step, block):
                    copy.wait()

        at = 0
        for piece in rows:
            count = piece.shape[0]
            value = jnp.dot(piece[...], held[step], preferred_element_type=F32)
            if with_arrived:
                value = value + arrived[step][at : at + count].astype(F32)
            outs[step][at : at + count] = value.astype(BF)
            at += count


def product(order, items, pieces, arrived, steps):
    rows = sum(piece.shape[0] for piece in items)
    depth, q = pieces[0][0].shape
    flat = [part for block in pieces for part in block]
    extra = list(arrived) if arrived is not None else []
    vmem = pl.BlockSpec(memory_space=pltpu.VMEM)
    return pl.pallas_call(
        functools.partial(
            product_kernel,
            items=len(items),
            pieces=tuple(len(block) for block in pieces),
            steps=steps,
            with_arrived=arrived is not None,
        ),
        in_specs=[pl.BlockSpec(memory_space=pltpu.SMEM)]
        + [vmem] * len(items)
        + [pl.BlockSpec(memory_space=pl.ANY)] * len(flat)
        + [vmem] * len(extra),
        out_specs=[vmem] * steps,
        out_shape=[jax.ShapeDtypeStruct((rows, q), BF)] * steps,
        scratch_shapes=[
            pltpu.VMEM((steps, depth, q), BF),
            pltpu.SemaphoreType.DMA((steps, 2)),
        ],
        compiler_params=pltpu.CompilerParams(vmem_limit_bytes=24 * 1024 * 1024),
        cost_estimate=pl.CostEstimate(
            flops=2 * rows * depth * q * steps,
            bytes_accessed=2 * (rows * depth + steps * (depth * q + rows * q)),
            transcendentals=0,
        ),
        name="product",
    )(order, *items, *flat, *extra)


def place_kernel(dests, *refs, sources, count, cap):
    *terms, out, total, used = refs
    value = terms[0][...].astype(F32)
    for term in terms[1:]:
        value = value + term[...].astype(F32)
    total[...] = value
    out[...] = jnp.zeros_like(out)
    peers = out.shape[0]
    rows = out.shape[2]
    for s in range(sources):

        @pl.loop(0, peers)
        def _(d):
            used[d] = 0

        @pl.loop(0, count)
        def _(j, s=s):
            d = dests[s * count + j]
            rank = used[d]
            used[d] = rank + 1
            start = pl.multiple_of((s * count + j) * rows, rows)
            out[d, s * cap + rank] = total[pl.ds(start, rows), :].astype(BF)


def place(dests, terms, peers, sources, count, cap, rows):
    q = terms[0].shape[1]
    shape = (peers, sources * cap, rows, q)
    return pl.pallas_call(
        functools.partial(place_kernel, sources=sources, count=count, cap=cap),
        grid_spec=pltpu.PrefetchScalarGridSpec(
            num_scalar_prefetch=1,
            grid=(1,),
            in_specs=[pl.BlockSpec(t.shape, lambda s, o: (0, 0)) for t in terms],
            out_specs=pl.BlockSpec(shape, lambda s, o: (0, 0, 0, 0)),
            scratch_shapes=[pltpu.VMEM(terms[0].shape, F32), pltpu.SMEM((peers,), jnp.int32)],
        ),
        out_shape=jax.ShapeDtypeStruct(shape, BF),
        compiler_params=params(),
        cost_estimate=pl.CostEstimate(
            flops=8 * terms[0].size, bytes_accessed=2 * (4 * terms[0].size + 2 * terms[0].size), transcendentals=0
        ),
        name="place",
    )(dests, *terms)


def final_kernel(*refs, offsets, cap):
    *parts, out = refs
    nx = parts[0].shape[0]
    q = parts[0].shape[3]
    for part, steps in zip(parts, offsets):
        for at, d in enumerate(steps):
            for x in range(nx):
                slot = ((x - d) % nx) * cap
                out[slot : slot + cap, :, x * q : (x + 1) * q] = part[x, at * cap : (at + 1) * cap]


def finish(parts, offsets, nz, nx, cap):
    peers, slots, rows, q = parts[0].shape
    return pl.pallas_call(
        functools.partial(final_kernel, offsets=offsets, cap=cap),
        grid=(nz,),
        in_specs=[pl.BlockSpec((nx, slots, rows, q), lambda s: (s, 0, 0, 0))] * len(parts),
        out_specs=pl.BlockSpec((nx * cap, rows, nx * q), lambda s: (s, 0, 0)),
        out_shape=jax.ShapeDtypeStruct((peers * cap, rows, nx * q), BF),
        compiler_params=params(),
        name="finish",
    )(*parts)


def per_device(integrals, occupied_coeffs, metric, mu_block, pair_count, destination):
    nz, nx, ny = lax.axis_size("z"), lax.axis_size("x"), lax.axis_size("y")
    peers = nz * nx
    count = destination.shape[0]
    cap = max(2, (2 * count + peers - 1) // peers)
    _, mu_width, nu, p_local = integrals.shape
    orbitals, local_width = occupied_coeffs.shape
    item_rows = nu * orbitals // count

    def hop(value, axis, size, step):
        return lax.ppermute(value, axis, shift(size, step))

    def after(value, *others):
        return lax.optimization_barrier((value,) + others)[0]

    mid = metric.shape[0] // 2
    up, down = [metric], [metric]
    for _ in range(nz // 2 - 1):
        up.append(hop(up[-1], "z", nz, 1))
        down.append(hop(down[-1], "z", nz, -1))
    far = (hop(up[-1][:mid], "z", nz, 1), hop(down[-1][mid:], "z", nz, -1))
    pieces = [(block,) for block in up] + [far] + [(block,) for block in down[:0:-1]]

    dest_row = jnp.pad(destination.astype(BF)[None], ((0, 8 - orbitals - 1), (0, local_width - count)))
    packed = jnp.concatenate([occupied_coeffs, dest_row], axis=0)
    packed = lax.all_to_all(
        jnp.broadcast_to(packed[None], (peers,) + packed.shape), ("z", "x"), 0, 0, tiled=True
    )
    blocks_per = local_width // mu_width
    where = jnp.stack([mu_block[0] // blocks_per, mu_block[0] % blocks_per, pair_count[0]])
    halves = half_transform(where, packed, integrals[0], orbitals)

    half = halves.shape[0] // 2
    ahead = hop(halves, "x", nx, 1)
    behind = hop(halves, "x", nx, -1)
    far_low = hop(ahead[:half], "x", nx, 1)
    far_high = hop(behind[half:], "x", nx, -1)
    items = (halves, ahead, behind, far_low, far_high)
    offsets = (0, 1, 3, 2)

    z, x, y, core = (lax.axis_index(name) for name in ("z", "x", "y", "core"))
    dests = packed[:, orbitals, :count].astype(jnp.int32)
    rows_of = jnp.concatenate(
        [lax.dynamic_index_in_dim(dests, z * nx + (x - d) % nx, 0, False) for d in offsets]
    )
    turns = ((2, 1), (3, 0))

    def order_of(turn, owner_core):
        return jnp.stack([(z - 2 * ((y + k) % ny) - owner_core) % nz for k in turn]).astype(jnp.int32)

    swap = [(0, 1), (1, 0)]
    swapped = []
    for turn in turns:
        other = product(order_of(turn, 1 - core), items, pieces, None, len(turn))
        swapped.append([lax.ppermute(value, "core", swap) for value in other])
    terms = {}
    for turn, arrived in zip(turns, swapped):
        own = product(order_of(turn, core), items, pieces, arrived, len(turn))
        for k, value in zip(turn, own):
            terms[k] = hop(value, "y", ny, k) if k else value
    outgoing = place(
        rows_of, [terms[k] for k in range(ny)], peers, len(offsets), count, cap, item_rows
    )
    arrived = lax.all_to_all(outgoing, ("z", "x"), 0, 0, tiled=True)
    return finish([arrived], [offsets], nz, nx, cap)


def solution(mesh):
    grid = mesh.devices.reshape(8, 4, mesh.shape["narrow"] // 2, 2)
    fine = Mesh(grid, ("z", "x", "y", "core"))
    wide, narrow = ("z", "x"), ("y", "core")
    placed = (
        P(wide, None, None, narrow),
        P(None, wide),
        P(narrow, wide),
        P(wide),
        P(wide),
        P(wide),
    )
    return jax.shard_map(
        per_device, mesh=fine, in_specs=placed, out_specs=P(wide, None, narrow), check_vma=False
    )
```

```python
import functools

import jax
import jax.numpy as jnp
from jax import lax
from jax.experimental import pallas as pl
from jax.experimental.pallas import tpu as pltpu
from jax.sharding import Mesh, PartitionSpec as P

BF = jnp.bfloat16
F32 = jnp.float32
VMEM_LIMIT = 48 * 1024 * 1024
SMALL_LIMIT = 24 * 1024 * 1024


def shift(size, step):
    return [(i, (i + step) % size) for i in range(size)]


def params(limit=VMEM_LIMIT):
    return pltpu.CompilerParams(vmem_limit_bytes=limit)


def halves_kernel(where, packed_ref, block_ref, out_ref, weight, *, orbitals):
    width, group, p = block_ref.shape
    rows, depth = group * orbitals, width * group
    lanes, packs = packed_ref.shape[2], packed_ref.shape[1]

    def iota(shape, dim):
        return lax.broadcasted_iota(jnp.int32, shape, dim)

    def dot(left, right):
        return jnp.dot(left, right, preferred_element_type=F32)

    pick = iota((lanes, width), 0) == where[1] * width + iota((lanes, width), 1)
    chosen = dot(packed_ref[0], pick.astype(BF)).astype(BF)
    repeat = lax.rem(iota((rows, packs), 0), orbitals) == iota((rows, packs), 1)
    coeff = dot(repeat.astype(BF), chosen).astype(BF)
    spread = iota((width, depth), 0) == iota((width, depth), 1) // group
    wide = dot(coeff, spread.astype(BF))
    row_nu = iota((rows, depth), 0) // orbitals
    col_nu = lax.rem(iota((rows, depth), 1), group)
    live = pl.program_id(0) * group + row_nu < where[2]
    weight[...] = jnp.where((row_nu == col_nu) & live, wide, 0.0).astype(BF)
    out_ref[...] = dot(weight[...], block_ref[...].reshape(depth, p)).astype(BF)


def half_transform(where, packed, block, orbitals):
    mu, nu, p = block.shape
    group = 32
    rows = group * orbitals
    return pl.pallas_call(
        functools.partial(halves_kernel, orbitals=orbitals),
        grid_spec=pltpu.PrefetchScalarGridSpec(
            num_scalar_prefetch=1,
            grid=(nu // group,),
            in_specs=[
                pl.BlockSpec((1,) + packed.shape[1:], lambda s, w: (w[0], 0, 0)),
                pl.BlockSpec((mu, group, p), lambda s, w: (0, s, 0)),
            ],
            out_specs=pl.BlockSpec((rows, p), lambda s, w: (s, 0)),
            scratch_shapes=[pltpu.VMEM((rows, mu * group), BF)],
        ),
        out_shape=jax.ShapeDtypeStruct((nu * orbitals, p), BF),
        compiler_params=params(),
        cost_estimate=pl.CostEstimate(
            flops=2 * rows * mu * nu * p, bytes_accessed=2 * mu * nu * p, transcendentals=0
        ),
        name="halves",
    )(where, packed, block)


def product_kernel(order, *refs, items, pieces, steps, adds, outs):
    refs = list(refs)
    rows = [refs.pop(0) for _ in range(items)]
    blocks = [[refs.pop(0) for _ in range(n)] for n in pieces]
    terms = [refs.pop(0) for _ in adds]
    results = [refs.pop(0) for _ in outs]
    held, sems, added, added_sems = refs

    def copies(step, block):
        at = 0
        for part, ref in enumerate(block):
            depth = ref.shape[0]
            yield pltpu.make_async_copy(ref, held.at[step, pl.ds(at, depth)], sems.at[step, part])
            at += depth

    def each(step, act):
        for d, block in enumerate(blocks):

            @pl.when(order[step] == d)
            def _(block=block):
                for copy in copies(step, block):
                    act(copy)

    def added_copy(slot):
        term = terms[slot] if adds[slot][0] is None else terms[slot].at[adds[slot][0]]
        spot = added.at[slot, pl.ds(0, term.shape[0])]
        return pltpu.make_async_copy(term, spot, added_sems.at[slot])

    for step in range(steps):
        each(step, lambda copy: copy.start())
        for slot, (_, wanted, _) in enumerate(adds):
            if wanted == step:
                added_copy(slot).start()

    for step in range(steps):
        each(step, lambda copy: copy.wait())
        for slot, (_, wanted, _) in enumerate(adds):
            if wanted == step:
                added_copy(slot).wait()
        at = 0
        for piece in rows:
            count = piece.shape[0]
            value = jnp.dot(piece[...], held[step], preferred_element_type=F32)
            for slot, (_, wanted, first) in enumerate(adds):
                size = terms[slot].shape[-2]
                if wanted == step and first <= at < first + size:
                    value = value + added[slot, at - first : at - first + count].astype(F32)
            for ref, places in zip(results, outs):
                for wanted, lead, first in places:
                    size = ref.shape[-2]
                    if wanted == step and first <= at < first + size:
                        spot = slice(at - first, at - first + count)
                        if lead is None:
                            ref[spot] = value.astype(BF)
                        else:
                            ref[lead, spot] = value.astype(BF)
            at += count


def product(order, items, pieces, terms, shapes, outs):
    rows = sum(piece.shape[0] for piece in items)
    depth, q = pieces[0][0].shape
    steps = order.shape[0]
    flat = [
        pltpu.with_memory_space_constraint(part, pltpu.HBM) for block in pieces for part in block
    ]
    hbm = pl.BlockSpec(memory_space=pltpu.HBM)
    vmem = pl.BlockSpec(memory_space=pltpu.VMEM)
    slots = max(1, len(terms))
    return pl.pallas_call(
        functools.partial(
            product_kernel,
            items=len(items),
            pieces=tuple(len(block) for block in pieces),
            steps=steps,
            adds=tuple(term[1:] for term in terms),
            outs=outs,
        ),
        in_specs=[pl.BlockSpec(memory_space=pltpu.SMEM)]
        + [vmem] * len(items)
        + [hbm] * (len(flat) + len(terms)),
        out_specs=[vmem] * len(shapes),
        out_shape=[jax.ShapeDtypeStruct(shape, BF) for shape in shapes],
        scratch_shapes=[
            pltpu.VMEM((steps, depth, q), BF),
            pltpu.SemaphoreType.DMA((steps, 2)),
            pltpu.VMEM((slots, rows if terms else 16, q), BF),
            pltpu.SemaphoreType.DMA((slots,)),
        ],
        compiler_params=params(SMALL_LIMIT),
        cost_estimate=pl.CostEstimate(
            flops=2 * rows * depth * q * steps,
            bytes_accessed=2 * (rows * depth + steps * (depth * q + rows * q)),
            transcendentals=0,
        ),
        name="product",
    )(order, *items, *flat, *[term[0] for term in terms])


def place_kernel(dests, *refs, sources, count, cap):
    *terms, out, total, used, held, sems = refs
    copies = [
        pltpu.make_async_copy(term, held.at[at], sems.at[at]) for at, term in enumerate(terms)
    ]
    for copy in copies:
        copy.start()
    out[...] = jnp.zeros_like(out)
    for copy in copies:
        copy.wait()
    value = held[0].astype(F32)
    for at in range(1, len(terms)):
        value = value + held[at].astype(F32)
    total[...] = value
    peers = out.shape[0]
    rows = out.shape[2]
    for s in range(sources):

        @pl.loop(0, peers)
        def _(d):
            used[d] = 0

        @pl.loop(0, count)
        def _(j, s=s):
            d = dests[s * count + j]
            rank = used[d]
            used[d] = rank + 1
            start = pl.multiple_of((s * count + j) * rows, rows)
            out[d, s * cap + rank] = total[pl.ds(start, rows), :].astype(BF)


def place(dests, terms, peers, sources, count, cap, rows):
    q = terms[0].shape[1]
    shape = (peers, sources * cap, rows, q)
    return pl.pallas_call(
        functools.partial(place_kernel, sources=sources, count=count, cap=cap),
        grid_spec=pltpu.PrefetchScalarGridSpec(
            num_scalar_prefetch=1,
            grid=(1,),
            in_specs=[pl.BlockSpec(memory_space=pltpu.HBM)] * len(terms),
            out_specs=pl.BlockSpec(shape, lambda s, o: (0, 0, 0, 0)),
            scratch_shapes=[
                pltpu.VMEM(terms[0].shape, F32),
                pltpu.SMEM((peers,), jnp.int32),
                pltpu.VMEM((len(terms),) + terms[0].shape, BF),
                pltpu.SemaphoreType.DMA((len(terms),)),
            ],
        ),
        out_shape=jax.ShapeDtypeStruct(shape, BF),
        compiler_params=params(SMALL_LIMIT),
        cost_estimate=pl.CostEstimate(
            flops=8 * terms[0].size, bytes_accessed=2 * (4 * terms[0].size + 2 * terms[0].size), transcendentals=0
        ),
        name="place",
    )(dests, *terms)


def final_kernel(part, out, *, offsets, nx, cap):
    q = part.shape[3]
    for z in range(part.shape[0] // nx):
        for at, d in enumerate(offsets):
            for x in range(nx):
                slot = (z * nx + (x - d) % nx) * cap
                out[slot : slot + cap, :, x * q : (x + 1) * q] = part[
                    z * nx + x, at * cap : (at + 1) * cap
                ]


def finish(arrived, offsets, nx, cap):
    peers, slots, rows, q = arrived.shape
    steps = 2
    return pl.pallas_call(
        functools.partial(final_kernel, offsets=offsets, nx=nx, cap=cap),
        grid=(steps,),
        in_specs=[pl.BlockSpec((peers // steps, slots, rows, q), lambda s: (s, 0, 0, 0))],
        out_specs=pl.BlockSpec((peers * cap // steps, rows, nx * q), lambda s: (s, 0, 0)),
        out_shape=jax.ShapeDtypeStruct((peers * cap, rows, nx * q), BF),
        compiler_params=params(SMALL_LIMIT),
        name="finish",
    )(arrived)


def per_device(integrals, occupied_coeffs, metric, mu_block, pair_count, destination):
    nz, nx, ny = lax.axis_size("z"), lax.axis_size("x"), lax.axis_size("y")
    peers = nz * nx
    count = destination.shape[0]
    cap = max(2, (2 * count + peers - 1) // peers)
    _, mu_width, nu, p_local = integrals.shape
    orbitals, local_width = occupied_coeffs.shape
    item_rows = nu * orbitals // count

    def hop(value, axis, size, step):
        return lax.ppermute(value, axis, shift(size, step))

    mid = metric.shape[0] // 2
    up, down = [metric], [metric]
    for _ in range(nz // 2 - 1):
        up.append(hop(up[-1], "z", nz, 1))
        down.append(hop(down[-1], "z", nz, -1))
    far = (hop(up[-1][:mid], "z", nz, 1), hop(down[-1][mid:], "z", nz, -1))
    pieces = [(block,) for block in up] + [far] + [(block,) for block in down[:0:-1]]

    dest_row = jnp.pad(destination.astype(BF)[None], ((0, 8 - orbitals - 1), (0, local_width - count)))
    packed = jnp.concatenate([occupied_coeffs, dest_row], axis=0)
    packed = lax.all_to_all(
        jnp.broadcast_to(packed[None], (peers,) + packed.shape), ("z", "x"), 0, 0, tiled=True
    )
    blocks_per = local_width // mu_width
    where = jnp.stack([mu_block[0] // blocks_per, mu_block[0] % blocks_per, pair_count[0]])
    halves = half_transform(where, packed, integrals[0], orbitals)

    half = halves.shape[0] // 2
    ahead = hop(halves, "x", nx, 1)
    behind = hop(halves, "x", nx, -1)
    far_low = hop(ahead[:half], "x", nx, 1)
    far_high = hop(behind[half:], "x", nx, -1)
    items = (halves, ahead, behind, far_low, far_high)
    offsets = (0, 1, 3, 2)

    z, x, y, core = (lax.axis_index(name) for name in ("z", "x", "y", "core"))
    dests = packed[:, orbitals, :count].astype(jnp.int32)
    rows_of = jnp.concatenate(
        [lax.dynamic_index_in_dim(dests, z * nx + (x - d) % nx, 0, False) for d in offsets]
    )
    def order_of(turn, owner_core):
        return jnp.stack([(z - 2 * ((y + k) % ny) - owner_core) % nz for k in turn]).astype(jnp.int32)

    rows, q = halves.shape[0] * nx, metric.shape[1]
    near = rows // 2
    swap = [(0, 1), (1, 0)]
    first, second = product(
        order_of((2, 0, 1, 3), 1 - core),
        items,
        pieces,
        (),
        ((2, rows, q), (2, rows, q)),
        (((0, 0, 0), (1, 1, 0)), ((2, 0, 0), (3, 1, 0))),
    )
    first = lax.ppermute(first, "core", swap)
    second = lax.ppermute(second, "core", swap)
    low, high = product(
        order_of((2,), core),
        items,
        pieces,
        ((first, 0, 0, 0),),
        ((near, q), (near, q)),
        (((0, None, 0),), ((0, None, near),)),
    )
    low, high = hop(low, "y", ny, -1), hop(high, "y", ny, 1)
    right, left = product(
        order_of((1, 3), core),
        items,
        pieces,
        ((second, 0, 0, 0), (second, 1, 1, 0), (high, None, 0, near), (low, None, 1, 0)),
        ((rows, q), (rows, q)),
        (((0, None, 0),), ((1, None, 0),)),
    )
    (kept,) = product(
        order_of((0,), core),
        items,
        pieces,
        ((first, 1, 0, 0),),
        ((rows, q),),
        (((0, None, 0),),),
    )
    terms = [kept, hop(right, "y", ny, 1), hop(left, "y", ny, -1)]
    outgoing = place(
        rows_of, terms, peers, len(offsets), count, cap, item_rows
    )
    arrived = lax.all_to_all(outgoing, ("z", "x"), 0, 0, tiled=True)
    return finish(arrived, offsets, nx, cap)


def solution(mesh):
    grid = mesh.devices.reshape(8, 4, mesh.shape["narrow"] // 2, 2)
    fine = Mesh(grid, ("z", "x", "y", "core"))
    wide, narrow = ("z", "x"), ("y", "core")
    placed = (
        P(wide, None, None, narrow),
        P(None, wide),
        P(narrow, wide),
        P(wide),
        P(wide),
        P(wide),
    )
    return jax.shard_map(
        per_device, mesh=fine, in_specs=placed, out_specs=P(wide, None, narrow), check_vma=False
    )
```

```python
import functools

import jax
import jax.numpy as jnp
from jax import lax
from jax.experimental import pallas as pl
from jax.experimental.pallas import tpu as pltpu
from jax.sharding import Mesh, PartitionSpec as P

BF = jnp.bfloat16
F32 = jnp.float32
VMEM_LIMIT = 48 * 1024 * 1024
SMALL_LIMIT = 24 * 1024 * 1024


def shift(size, step):
    return [(i, (i + step) % size) for i in range(size)]


def params(limit=VMEM_LIMIT):
    return pltpu.CompilerParams(vmem_limit_bytes=limit)


def halves_kernel(where, packed_ref, block_ref, out_ref, weight, *, orbitals):
    width, group, p = block_ref.shape
    rows, depth = group * orbitals, width * group
    lanes, packs = packed_ref.shape[2], packed_ref.shape[1]

    def iota(shape, dim):
        return lax.broadcasted_iota(jnp.int32, shape, dim)

    def dot(left, right):
        return jnp.dot(left, right, preferred_element_type=F32)

    pick = iota((lanes, width), 0) == where[1] * width + iota((lanes, width), 1)
    chosen = dot(packed_ref[0], pick.astype(BF)).astype(BF)
    repeat = lax.rem(iota((rows, packs), 0), orbitals) == iota((rows, packs), 1)
    coeff = dot(repeat.astype(BF), chosen).astype(BF)
    spread = iota((width, depth), 0) == iota((width, depth), 1) // group
    wide = dot(coeff, spread.astype(BF))
    row_nu = iota((rows, depth), 0) // orbitals
    col_nu = lax.rem(iota((rows, depth), 1), group)
    live = pl.program_id(0) * group + row_nu < where[2]
    weight[...] = jnp.where((row_nu == col_nu) & live, wide, 0.0).astype(BF)
    out_ref[...] = dot(weight[...], block_ref[...].reshape(depth, p)).astype(BF)


def half_transform(where, packed, block, orbitals):
    mu, nu, p = block.shape
    group = 32
    rows = group * orbitals
    return pl.pallas_call(
        functools.partial(halves_kernel, orbitals=orbitals),
        grid_spec=pltpu.PrefetchScalarGridSpec(
            num_scalar_prefetch=1,
            grid=(nu // group,),
            in_specs=[
                pl.BlockSpec((1,) + packed.shape[1:], lambda s, w: (w[0], 0, 0)),
                pl.BlockSpec((mu, group, p), lambda s, w: (0, s, 0)),
            ],
            out_specs=pl.BlockSpec((rows, p), lambda s, w: (s, 0)),
            scratch_shapes=[pltpu.VMEM((rows, mu * group), BF)],
        ),
        out_shape=jax.ShapeDtypeStruct((nu * orbitals, p), BF),
        compiler_params=params(),
        cost_estimate=pl.CostEstimate(
            flops=2 * rows * mu * nu * p, bytes_accessed=2 * mu * nu * p, transcendentals=0
        ),
        name="halves",
    )(where, packed, block)


def product_kernel(order, *refs, items, pieces, steps, adds, outs):
    refs = list(refs)
    rows = [refs.pop(0) for _ in range(items)]
    blocks = [[refs.pop(0) for _ in range(n)] for n in pieces]
    terms = [refs.pop(0) for _ in adds]
    results = [refs.pop(0) for _ in outs]
    held, sems, added, added_sems = refs

    def copies(step, block):
        at = 0
        for part, ref in enumerate(block):
            depth = ref.shape[0]
            yield pltpu.make_async_copy(ref, held.at[step, pl.ds(at, depth)], sems.at[step, part])
            at += depth

    def each(step, act):
        for d, block in enumerate(blocks):

            @pl.when(order[step] == d)
            def _(block=block):
                for copy in copies(step, block):
                    act(copy)

    def added_copy(slot):
        term = terms[slot] if adds[slot][0] is None else terms[slot].at[adds[slot][0]]
        spot = added.at[slot, pl.ds(0, term.shape[0])]
        return pltpu.make_async_copy(term, spot, added_sems.at[slot])

    for step in range(steps):
        each(step, lambda copy: copy.start())
        for slot, (_, wanted, _) in enumerate(adds):
            if wanted == step:
                added_copy(slot).start()

    for step in range(steps):
        each(step, lambda copy: copy.wait())
        for slot, (_, wanted, _) in enumerate(adds):
            if wanted == step:
                added_copy(slot).wait()
        at = 0
        for piece in rows:
            count = piece.shape[0]
            if not any(
                wanted == step and first <= at < first + ref.shape[-2]
                for ref, places in zip(results, outs)
                for wanted, _, first in places
            ):
                at += count
                continue
            value = jnp.dot(piece[...], held[step], preferred_element_type=F32)
            for slot, (_, wanted, first) in enumerate(adds):
                size = terms[slot].shape[-2]
                if wanted == step and first <= at < first + size:
                    value = value + added[slot, at - first : at - first + count].astype(F32)
            for ref, places in zip(results, outs):
                for wanted, lead, first in places:
                    size = ref.shape[-2]
                    if wanted == step and first <= at < first + size:
                        spot = slice(at - first, at - first + count)
                        if lead is None:
                            ref[spot] = value.astype(BF)
                        else:
                            ref[lead, spot] = value.astype(BF)
            at += count


def product(order, items, pieces, terms, shapes, outs):
    rows = sum(piece.shape[0] for piece in items)
    depth, q = pieces[0][0].shape
    steps = order.shape[0]
    flat = [
        pltpu.with_memory_space_constraint(part, pltpu.HBM) for block in pieces for part in block
    ]
    hbm = pl.BlockSpec(memory_space=pltpu.HBM)
    vmem = pl.BlockSpec(memory_space=pltpu.VMEM)
    slots = max(1, len(terms))
    return pl.pallas_call(
        functools.partial(
            product_kernel,
            items=len(items),
            pieces=tuple(len(block) for block in pieces),
            steps=steps,
            adds=tuple(term[1:] for term in terms),
            outs=outs,
        ),
        in_specs=[pl.BlockSpec(memory_space=pltpu.SMEM)]
        + [vmem] * len(items)
        + [hbm] * (len(flat) + len(terms)),
        out_specs=[vmem] * len(shapes),
        out_shape=[jax.ShapeDtypeStruct(shape, BF) for shape in shapes],
        scratch_shapes=[
            pltpu.VMEM((steps, depth, q), BF),
            pltpu.SemaphoreType.DMA((steps, 2)),
            pltpu.VMEM((slots, rows if terms else 16, q), BF),
            pltpu.SemaphoreType.DMA((slots,)),
        ],
        compiler_params=params(SMALL_LIMIT),
        cost_estimate=pl.CostEstimate(
            flops=2 * rows * depth * q * steps,
            bytes_accessed=2 * (rows * depth + steps * (depth * q + rows * q)),
            transcendentals=0,
        ),
        name="product",
    )(order, *items, *flat, *[term[0] for term in terms])


def place_kernel(dests, *refs, sources, count, cap, parts):
    refs = list(refs)
    terms = [[refs.pop(0) for _ in range(n)] for n in parts]
    out, total, used, held, sems = refs
    copies = []
    for at, term in enumerate(terms):
        row = 0
        for part, ref in enumerate(term):
            spot = held.at[at, pl.ds(row, ref.shape[0])]
            copies.append(pltpu.make_async_copy(ref, spot, sems.at[at, part]))
            row += ref.shape[0]
    for copy in copies:
        copy.start()
    out[...] = jnp.zeros_like(out)
    for copy in copies:
        copy.wait()
    value = held[0].astype(F32)
    for at in range(1, len(parts)):
        value = value + held[at].astype(F32)
    total[...] = value
    peers = out.shape[0]
    rows = out.shape[2]
    for s in range(sources):

        @pl.loop(0, peers)
        def _(d):
            used[d] = 0

        @pl.loop(0, count)
        def _(j, s=s):
            d = dests[s * count + j]
            rank = used[d]
            used[d] = rank + 1
            start = pl.multiple_of((s * count + j) * rows, rows)
            out[d, s * cap + rank] = total[pl.ds(start, rows), :].astype(BF)


def place(dests, terms, peers, sources, count, cap, rows):
    flat = [part for term in terms for part in term]
    q = flat[0].shape[1]
    shape = (peers, sources * cap, rows, q)
    size = sources * count * rows
    return pl.pallas_call(
        functools.partial(
            place_kernel,
            sources=sources,
            count=count,
            cap=cap,
            parts=tuple(len(term) for term in terms),
        ),
        grid_spec=pltpu.PrefetchScalarGridSpec(
            num_scalar_prefetch=1,
            grid=(1,),
            in_specs=[pl.BlockSpec(memory_space=pltpu.HBM)] * len(flat),
            out_specs=pl.BlockSpec(shape, lambda s, o: (0, 0, 0, 0)),
            scratch_shapes=[
                pltpu.VMEM((size, q), F32),
                pltpu.SMEM((peers,), jnp.int32),
                pltpu.VMEM((len(terms), size, q), BF),
                pltpu.SemaphoreType.DMA((len(terms), 2)),
            ],
        ),
        out_shape=jax.ShapeDtypeStruct(shape, BF),
        compiler_params=params(SMALL_LIMIT),
        cost_estimate=pl.CostEstimate(
            flops=4 * size * q, bytes_accessed=10 * size * q, transcendentals=0
        ),
        name="place",
    )(dests, *flat)


def final_kernel(part, out, *, offsets, nx, cap):
    q = part.shape[3]
    for z in range(part.shape[0] // nx):
        for at, d in enumerate(offsets):
            for x in range(nx):
                slot = (z * nx + (x - d) % nx) * cap
                out[slot : slot + cap, :, x * q : (x + 1) * q] = part[
                    z * nx + x, at * cap : (at + 1) * cap
                ]


def finish(arrived, offsets, nx, cap):
    peers, slots, rows, q = arrived.shape
    steps = 2
    return pl.pallas_call(
        functools.partial(final_kernel, offsets=offsets, nx=nx, cap=cap),
        grid=(steps,),
        in_specs=[pl.BlockSpec((peers // steps, slots, rows, q), lambda s: (s, 0, 0, 0))],
        out_specs=pl.BlockSpec((peers * cap // steps, rows, nx * q), lambda s: (s, 0, 0)),
        out_shape=jax.ShapeDtypeStruct((peers * cap, rows, nx * q), BF),
        compiler_params=params(SMALL_LIMIT),
        name="finish",
    )(arrived)


def per_device(integrals, occupied_coeffs, metric, mu_block, pair_count, destination):
    nz, nx, ny = lax.axis_size("z"), lax.axis_size("x"), lax.axis_size("y")
    peers = nz * nx
    count = destination.shape[0]
    cap = max(2, (2 * count + peers - 1) // peers)
    _, mu_width, nu, p_local = integrals.shape
    orbitals, local_width = occupied_coeffs.shape
    item_rows = nu * orbitals // count

    def hop(value, axis, size, step):
        return lax.ppermute(value, axis, shift(size, step))

    mid = metric.shape[0] // 2
    up, down = [metric], [metric]
    for _ in range(nz // 2 - 1):
        up.append(hop(up[-1], "z", nz, 1))
        down.append(hop(down[-1], "z", nz, -1))
    far = (hop(up[-1][:mid], "z", nz, 1), hop(down[-1][mid:], "z", nz, -1))
    pieces = [(block,) for block in up] + [far] + [(block,) for block in down[:0:-1]]

    dest_row = jnp.pad(destination.astype(BF)[None], ((0, 8 - orbitals - 1), (0, local_width - count)))
    packed = jnp.concatenate([occupied_coeffs, dest_row], axis=0)
    packed = lax.all_to_all(
        jnp.broadcast_to(packed[None], (peers,) + packed.shape), ("z", "x"), 0, 0, tiled=True
    )
    blocks_per = local_width // mu_width
    where = jnp.stack([mu_block[0] // blocks_per, mu_block[0] % blocks_per, pair_count[0]])
    halves = half_transform(where, packed, integrals[0], orbitals)

    half = halves.shape[0] // 2
    ahead = hop(halves, "x", nx, 1)
    behind = hop(halves, "x", nx, -1)
    far_low = hop(ahead[:half], "x", nx, 1)
    far_high = hop(behind[half:], "x", nx, -1)
    items = (halves, ahead, behind, far_low, far_high)
    offsets = (0, 1, 3, 2)

    z, x, y, core = (lax.axis_index(name) for name in ("z", "x", "y", "core"))
    dests = packed[:, orbitals, :count].astype(jnp.int32)
    rows_of = jnp.concatenate(
        [lax.dynamic_index_in_dim(dests, z * nx + (x - d) % nx, 0, False) for d in offsets]
    )
    def order_of(turn, owner_core):
        return jnp.stack([(z - 2 * ((y + k) % ny) - owner_core) % nz for k in turn]).astype(jnp.int32)

    rows, q = halves.shape[0] * nx, metric.shape[1]
    near = rows // 2
    swap = [(0, 1), (1, 0)]
    first, second = product(
        order_of((2, 0, 1, 3), 1 - core),
        items,
        pieces,
        (),
        ((2, rows, q), (2, rows, q)),
        (((0, 0, 0), (1, 1, 0)), ((2, 0, 0), (3, 1, 0))),
    )
    first = lax.ppermute(first, "core", swap)
    second = lax.ppermute(second, "core", swap)
    low, high = product(
        order_of((2,), core),
        items,
        pieces,
        ((first, 0, 0, 0),),
        ((near, q), (near, q)),
        (((0, None, 0),), ((0, None, near),)),
    )
    made = low
    low, high = hop(low, "y", ny, -1), hop(high, "y", ny, 1)
    right_low, left_high = product(
        lax.optimization_barrier((order_of((1, 3), core), made))[0],
        items,
        pieces,
        ((second, 0, 0, 0), (second, 1, 1, 0)),
        ((near, q), (near, q)),
        (((0, None, 0),), ((1, None, near),)),
    )
    right_high, left_low = product(
        order_of((1, 3), core),
        items,
        pieces,
        ((second, 0, 0, 0), (second, 1, 1, 0), (high, None, 0, near), (low, None, 1, 0)),
        ((near, q), (near, q)),
        (((0, None, near),), ((1, None, 0),)),
    )
    (kept,) = product(
        order_of((0,), core),
        items,
        pieces,
        ((first, 1, 0, 0),),
        ((rows, q),),
        (((0, None, 0),),),
    )
    terms = [
        (kept,),
        (hop(right_low, "y", ny, 1), hop(right_high, "y", ny, 1)),
        (hop(left_low, "y", ny, -1), hop(left_high, "y", ny, -1)),
    ]
    outgoing = place(
        rows_of, terms, peers, len(offsets), count, cap, item_rows
    )
    arrived = lax.all_to_all(outgoing, ("z", "x"), 0, 0, tiled=True)
    return finish(arrived, offsets, nx, cap)


def solution(mesh):
    grid = mesh.devices.reshape(8, 4, mesh.shape["narrow"] // 2, 2)
    fine = Mesh(grid, ("z", "x", "y", "core"))
    wide, narrow = ("z", "x"), ("y", "core")
    placed = (
        P(wide, None, None, narrow),
        P(None, wide),
        P(narrow, wide),
        P(wide),
        P(wide),
        P(wide),
    )
    return jax.shard_map(
        per_device, mesh=fine, in_specs=placed, out_specs=P(wide, None, narrow), check_vma=False
    )
```

```python
import functools

import jax
import jax.numpy as jnp
from jax import lax
from jax.experimental import pallas as pl
from jax.experimental.pallas import tpu as pltpu
from jax.sharding import Mesh, PartitionSpec as P

BF = jnp.bfloat16
F32 = jnp.float32
VMEM_LIMIT = 48 * 1024 * 1024
SMALL_LIMIT = 24 * 1024 * 1024


def shift(size, step):
    return [(i, (i + step) % size) for i in range(size)]


def params(limit=VMEM_LIMIT):
    return pltpu.CompilerParams(vmem_limit_bytes=limit)


def halves_kernel(where, packed_ref, block_ref, out_ref, weight, *, orbitals):
    width, group, p = block_ref.shape
    rows, depth = group * orbitals, width * group
    lanes, packs = packed_ref.shape[2], packed_ref.shape[1]

    def iota(shape, dim):
        return lax.broadcasted_iota(jnp.int32, shape, dim)

    def dot(left, right):
        return jnp.dot(left, right, preferred_element_type=F32)

    pick = iota((lanes, width), 0) == where[1] * width + iota((lanes, width), 1)
    chosen = dot(packed_ref[0], pick.astype(BF)).astype(BF)
    repeat = lax.rem(iota((rows, packs), 0), orbitals) == iota((rows, packs), 1)
    coeff = dot(repeat.astype(BF), chosen).astype(BF)
    spread = iota((width, depth), 0) == iota((width, depth), 1) // group
    wide = dot(coeff, spread.astype(BF))
    row_nu = iota((rows, depth), 0) // orbitals
    col_nu = lax.rem(iota((rows, depth), 1), group)
    live = pl.program_id(0) * group + row_nu < where[2]
    weight[...] = jnp.where((row_nu == col_nu) & live, wide, 0.0).astype(BF)
    out_ref[...] = dot(weight[...], block_ref[...].reshape(depth, p)).astype(BF)


def half_transform(where, packed, block, orbitals):
    mu, nu, p = block.shape
    group = 32
    rows = group * orbitals
    return pl.pallas_call(
        functools.partial(halves_kernel, orbitals=orbitals),
        grid_spec=pltpu.PrefetchScalarGridSpec(
            num_scalar_prefetch=1,
            grid=(nu // group,),
            in_specs=[
                pl.BlockSpec((1,) + packed.shape[1:], lambda s, w: (w[0], 0, 0)),
                pl.BlockSpec((mu, group, p), lambda s, w: (0, s, 0)),
            ],
            out_specs=pl.BlockSpec((rows, p), lambda s, w: (s, 0)),
            scratch_shapes=[pltpu.VMEM((rows, mu * group), BF)],
        ),
        out_shape=jax.ShapeDtypeStruct((nu * orbitals, p), BF),
        compiler_params=params(),
        cost_estimate=pl.CostEstimate(
            flops=2 * rows * mu * nu * p, bytes_accessed=2 * mu * nu * p, transcendentals=0
        ),
        name="halves",
    )(where, packed, block)


def product_kernel(order, *refs, items, pieces, steps, adds, outs):
    refs = list(refs)
    rows = [refs.pop(0) for _ in range(items)]
    blocks = [[refs.pop(0) for _ in range(n)] for n in pieces]
    terms = [refs.pop(0) for _ in adds]
    results = [refs.pop(0) for _ in outs]
    held, sems, added, added_sems = refs

    def copies(step, block):
        at = 0
        for part, ref in enumerate(block):
            depth = ref.shape[0]
            yield pltpu.make_async_copy(ref, held.at[step, pl.ds(at, depth)], sems.at[step, part])
            at += depth

    def each(step, act):
        for d, block in enumerate(blocks):

            @pl.when(order[step] == d)
            def _(block=block):
                for copy in copies(step, block):
                    act(copy)

    def added_copy(slot):
        term = terms[slot] if adds[slot][0] is None else terms[slot].at[adds[slot][0]]
        spot = added.at[slot, pl.ds(0, term.shape[0])]
        return pltpu.make_async_copy(term, spot, added_sems.at[slot])

    for step in range(steps):
        each(step, lambda copy: copy.start())
        for slot, (_, wanted, _) in enumerate(adds):
            if wanted == step:
                added_copy(slot).start()

    for step in range(steps):
        each(step, lambda copy: copy.wait())
        for slot, (_, wanted, _) in enumerate(adds):
            if wanted == step:
                added_copy(slot).wait()
        at = 0
        for piece in rows:
            count = piece.shape[0]
            if not any(
                wanted == step and first <= at < first + ref.shape[-2]
                for ref, places in zip(results, outs)
                for wanted, _, first in places
            ):
                at += count
                continue
            value = jnp.dot(piece[...], held[step], preferred_element_type=F32)
            for slot, (_, wanted, first) in enumerate(adds):
                size = terms[slot].shape[-2]
                if wanted == step and first <= at < first + size:
                    value = value + added[slot, at - first : at - first + count].astype(F32)
            for ref, places in zip(results, outs):
                for wanted, lead, first in places:
                    size = ref.shape[-2]
                    if wanted == step and first <= at < first + size:
                        spot = slice(at - first, at - first + count)
                        if lead is None:
                            ref[spot] = value.astype(BF)
                        else:
                            ref[lead, spot] = value.astype(BF)
            at += count


def product(order, items, pieces, terms, shapes, outs):
    rows = sum(piece.shape[0] for piece in items)
    depth, q = pieces[0][0].shape
    steps = order.shape[0]
    flat = [
        pltpu.with_memory_space_constraint(part, pltpu.HBM) for block in pieces for part in block
    ]
    hbm = pl.BlockSpec(memory_space=pltpu.HBM)
    vmem = pl.BlockSpec(memory_space=pltpu.VMEM)
    slots = max(1, len(terms))
    return pl.pallas_call(
        functools.partial(
            product_kernel,
            items=len(items),
            pieces=tuple(len(block) for block in pieces),
            steps=steps,
            adds=tuple(term[1:] for term in terms),
            outs=outs,
        ),
        in_specs=[pl.BlockSpec(memory_space=pltpu.SMEM)]
        + [vmem] * len(items)
        + [hbm] * (len(flat) + len(terms)),
        out_specs=[vmem] * len(shapes),
        out_shape=[jax.ShapeDtypeStruct(shape, BF) for shape in shapes],
        scratch_shapes=[
            pltpu.VMEM((steps, depth, q), BF),
            pltpu.SemaphoreType.DMA((steps, 2)),
            pltpu.VMEM((slots, rows if terms else 16, q), BF),
            pltpu.SemaphoreType.DMA((slots,)),
        ],
        compiler_params=params(SMALL_LIMIT),
        cost_estimate=pl.CostEstimate(
            flops=2 * rows * depth * q * steps,
            bytes_accessed=2 * (rows * depth + steps * (depth * q + rows * q)),
            transcendentals=0,
        ),
        name="product",
    )(order, *items, *flat, *[term[0] for term in terms])


def place_kernel(dests, *refs, sources, count, cap, parts):
    refs = list(refs)
    terms = [[refs.pop(0) for _ in range(n)] for n in parts]
    out, total, used, held, sems = refs
    copies = []
    for at, term in enumerate(terms):
        row = 0
        for part, ref in enumerate(term):
            spot = held.at[at, pl.ds(row, ref.shape[0])]
            copies.append(pltpu.make_async_copy(ref, spot, sems.at[at, part]))
            row += ref.shape[0]
    for copy in copies:
        copy.start()
    out[...] = jnp.zeros_like(out)
    for copy in copies:
        copy.wait()
    value = held[0].astype(F32)
    for at in range(1, len(parts)):
        value = value + held[at].astype(F32)
    total[...] = value
    peers = out.shape[0]
    rows = out.shape[2]
    for s in range(sources):

        @pl.loop(0, peers, unroll=8)
        def _(d):
            used[d] = 0

        @pl.loop(0, count, unroll=8)
        def _(j, s=s):
            d = dests[s * count + j]
            rank = used[d]
            used[d] = rank + 1
            start = pl.multiple_of((s * count + j) * rows, rows)
            out[d, s * cap + rank] = total[pl.ds(start, rows), :].astype(BF)


def place(dests, terms, peers, sources, count, cap, rows):
    flat = [part for term in terms for part in term]
    q = flat[0].shape[1]
    shape = (peers, sources * cap, rows, q)
    size = sources * count * rows
    return pl.pallas_call(
        functools.partial(
            place_kernel,
            sources=sources,
            count=count,
            cap=cap,
            parts=tuple(len(term) for term in terms),
        ),
        grid_spec=pltpu.PrefetchScalarGridSpec(
            num_scalar_prefetch=1,
            grid=(1,),
            in_specs=[pl.BlockSpec(memory_space=pltpu.HBM)] * len(flat),
            out_specs=pl.BlockSpec(shape, lambda s, o: (0, 0, 0, 0)),
            scratch_shapes=[
                pltpu.VMEM((size, q), F32),
                pltpu.SMEM((peers,), jnp.int32),
                pltpu.VMEM((len(terms), size, q), BF),
                pltpu.SemaphoreType.DMA((len(terms), 2)),
            ],
        ),
        out_shape=jax.ShapeDtypeStruct(shape, BF),
        compiler_params=params(SMALL_LIMIT),
        cost_estimate=pl.CostEstimate(
            flops=4 * size * q, bytes_accessed=10 * size * q, transcendentals=0
        ),
        name="place",
    )(dests, *flat)


def final_kernel(part, out, *, offsets, nx, cap):
    q = part.shape[3]
    for z in range(part.shape[0] // nx):
        for at, d in enumerate(offsets):
            for x in range(nx):
                slot = (z * nx + (x - d) % nx) * cap
                out[slot : slot + cap, :, x * q : (x + 1) * q] = part[
                    z * nx + x, at * cap : (at + 1) * cap
                ]


def finish(arrived, offsets, nx, cap):
    peers, slots, rows, q = arrived.shape
    steps = 2
    return pl.pallas_call(
        functools.partial(final_kernel, offsets=offsets, nx=nx, cap=cap),
        grid=(steps,),
        in_specs=[pl.BlockSpec((peers // steps, slots, rows, q), lambda s: (s, 0, 0, 0))],
        out_specs=pl.BlockSpec((peers * cap // steps, rows, nx * q), lambda s: (s, 0, 0)),
        out_shape=jax.ShapeDtypeStruct((peers * cap, rows, nx * q), BF),
        compiler_params=params(SMALL_LIMIT),
        name="finish",
    )(arrived)


def per_device(integrals, occupied_coeffs, metric, mu_block, pair_count, destination):
    nz, nx, ny = lax.axis_size("z"), lax.axis_size("x"), lax.axis_size("y")
    peers = nz * nx
    count = destination.shape[0]
    cap = max(2, (2 * count + peers - 1) // peers)
    _, mu_width, nu, p_local = integrals.shape
    orbitals, local_width = occupied_coeffs.shape
    item_rows = nu * orbitals // count

    def hop(value, axis, size, step):
        return lax.ppermute(value, axis, shift(size, step))

    mid = metric.shape[0] // 2
    up, down = [metric], [metric]
    for _ in range(nz // 2 - 1):
        up.append(hop(up[-1], "z", nz, 1))
        down.append(hop(down[-1], "z", nz, -1))
    far = (hop(up[-1][:mid], "z", nz, 1), hop(down[-1][mid:], "z", nz, -1))
    pieces = [(block,) for block in up] + [far] + [(block,) for block in down[:0:-1]]

    dest_row = jnp.pad(destination.astype(BF)[None], ((0, 8 - orbitals - 1), (0, local_width - count)))
    packed = jnp.concatenate([occupied_coeffs, dest_row], axis=0)
    packed = lax.all_to_all(
        jnp.broadcast_to(packed[None], (peers,) + packed.shape), ("z", "x"), 0, 0, tiled=True
    )
    blocks_per = local_width // mu_width
    where = jnp.stack([mu_block[0] // blocks_per, mu_block[0] % blocks_per, pair_count[0]])
    halves = half_transform(where, packed, integrals[0], orbitals)

    half = halves.shape[0] // 2
    ahead = hop(halves, "x", nx, 1)
    behind = hop(halves, "x", nx, -1)
    far_low = hop(ahead[:half], "x", nx, 1)
    far_high = hop(behind[half:], "x", nx, -1)
    items = (halves, ahead, behind, far_low, far_high)
    offsets = (0, 1, 3, 2)

    z, x, y, core = (lax.axis_index(name) for name in ("z", "x", "y", "core"))
    dests = packed[:, orbitals, :count].astype(jnp.int32)
    rows_of = jnp.concatenate(
        [lax.dynamic_index_in_dim(dests, z * nx + (x - d) % nx, 0, False) for d in offsets]
    )
    def order_of(turn, owner_core):
        return jnp.stack([(z - 2 * ((y + k) % ny) - owner_core) % nz for k in turn]).astype(jnp.int32)

    rows, q = halves.shape[0] * nx, metric.shape[1]
    near = rows // 2
    swap = [(0, 1), (1, 0)]
    first, second = product(
        order_of((2, 0, 1, 3), 1 - core),
        items,
        pieces,
        (),
        ((2, rows, q), (2, rows, q)),
        (((0, 0, 0), (1, 1, 0)), ((2, 0, 0), (3, 1, 0))),
    )
    first = lax.ppermute(first, "core", swap)
    second = lax.ppermute(second, "core", swap)
    low, high = product(
        order_of((2,), core),
        items,
        pieces,
        ((first, 0, 0, 0),),
        ((near, q), (near, q)),
        (((0, None, 0),), ((0, None, near),)),
    )
    made = low
    low, high = hop(low, "y", ny, -1), hop(high, "y", ny, 1)
    right_low, left_high = product(
        lax.optimization_barrier((order_of((1, 3), core), made))[0],
        items,
        pieces,
        ((second, 0, 0, 0), (second, 1, 1, 0)),
        ((near, q), (near, q)),
        (((0, None, 0),), ((1, None, near),)),
    )
    right_high, left_low = product(
        order_of((1, 3), core),
        items,
        pieces,
        ((second, 0, 0, 0), (second, 1, 1, 0), (high, None, 0, near), (low, None, 1, 0)),
        ((near, q), (near, q)),
        (((0, None, near),), ((1, None, 0),)),
    )
    (kept,) = product(
        order_of((0,), core),
        items,
        pieces,
        ((first, 1, 0, 0),),
        ((rows, q),),
        (((0, None, 0),),),
    )
    terms = [
        (kept,),
        (hop(right_low, "y", ny, 1), hop(right_high, "y", ny, 1)),
        (hop(left_low, "y", ny, -1), hop(left_high, "y", ny, -1)),
    ]
    outgoing = place(
        rows_of, terms, peers, len(offsets), count, cap, item_rows
    )
    arrived = lax.all_to_all(outgoing, ("z", "x"), 0, 0, tiled=True)
    return finish(arrived, offsets, nx, cap)


def solution(mesh):
    grid = mesh.devices.reshape(8, 4, mesh.shape["narrow"] // 2, 2)
    fine = Mesh(grid, ("z", "x", "y", "core"))
    wide, narrow = ("z", "x"), ("y", "core")
    placed = (
        P(wide, None, None, narrow),
        P(None, wide),
        P(narrow, wide),
        P(wide),
        P(wide),
        P(wide),
    )
    return jax.shard_map(
        per_device, mesh=fine, in_specs=placed, out_specs=P(wide, None, narrow), check_vma=False
    )
```

```python
import functools

import jax
import jax.numpy as jnp
from jax import lax
from jax.experimental import pallas as pl
from jax.experimental.pallas import tpu as pltpu
from jax.sharding import Mesh, PartitionSpec as P

BF = jnp.bfloat16
F32 = jnp.float32
VMEM_LIMIT = 48 * 1024 * 1024
SMALL_LIMIT = 24 * 1024 * 1024


def shift(size, step):
    return [(i, (i + step) % size) for i in range(size)]


def params(limit=VMEM_LIMIT):
    return pltpu.CompilerParams(vmem_limit_bytes=limit)


def halves_kernel(where, packed_ref, block_ref, out_ref, weight, *, orbitals):
    width, group, p = block_ref.shape
    rows, depth = group * orbitals, width * group
    lanes, packs = packed_ref.shape[2], packed_ref.shape[1]

    def iota(shape, dim):
        return lax.broadcasted_iota(jnp.int32, shape, dim)

    def dot(left, right):
        return jnp.dot(left, right, preferred_element_type=F32)

    pick = iota((lanes, width), 0) == where[1] * width + iota((lanes, width), 1)
    chosen = dot(packed_ref[0], pick.astype(BF)).astype(BF)
    repeat = lax.rem(iota((rows, packs), 0), orbitals) == iota((rows, packs), 1)
    coeff = dot(repeat.astype(BF), chosen).astype(BF)
    spread = iota((width, depth), 0) == iota((width, depth), 1) // group
    wide = dot(coeff, spread.astype(BF))
    row_nu = iota((rows, depth), 0) // orbitals
    col_nu = lax.rem(iota((rows, depth), 1), group)
    live = pl.program_id(0) * group + row_nu < where[2]
    weight[...] = jnp.where((row_nu == col_nu) & live, wide, 0.0).astype(BF)
    out_ref[...] = dot(weight[...], block_ref[...].reshape(depth, p)).astype(BF)


def half_transform(where, packed, block, orbitals):
    mu, nu, p = block.shape
    group = 32
    rows = group * orbitals
    return pl.pallas_call(
        functools.partial(halves_kernel, orbitals=orbitals),
        grid_spec=pltpu.PrefetchScalarGridSpec(
            num_scalar_prefetch=1,
            grid=(nu // group,),
            in_specs=[
                pl.BlockSpec((1,) + packed.shape[1:], lambda s, w: (w[0], 0, 0)),
                pl.BlockSpec((mu, group, p), lambda s, w: (0, s, 0)),
            ],
            out_specs=pl.BlockSpec((rows, p), lambda s, w: (s, 0)),
            scratch_shapes=[pltpu.VMEM((rows, mu * group), BF)],
        ),
        out_shape=jax.ShapeDtypeStruct((nu * orbitals, p), BF),
        compiler_params=params(),
        cost_estimate=pl.CostEstimate(
            flops=2 * rows * mu * nu * p, bytes_accessed=2 * mu * nu * p, transcendentals=0
        ),
        name="halves",
    )(where, packed, block)


def product_kernel(order, *refs, items, pieces, steps, adds, outs):
    refs = list(refs)
    rows = [refs.pop(0) for _ in range(items)]
    blocks = [[refs.pop(0) for _ in range(n)] for n in pieces]
    terms = [refs.pop(0) for _ in adds]
    results = [refs.pop(0) for _ in outs]
    held, sems, added, added_sems = refs

    def copies(step, block):
        at = 0
        for part, ref in enumerate(block):
            depth = ref.shape[0]
            yield pltpu.make_async_copy(ref, held.at[step, pl.ds(at, depth)], sems.at[step, part])
            at += depth

    def each(step, act):
        for d, block in enumerate(blocks):

            @pl.when(order[step] == d)
            def _(block=block):
                for copy in copies(step, block):
                    act(copy)

    def added_copy(slot):
        term = terms[slot] if adds[slot][0] is None else terms[slot].at[adds[slot][0]]
        spot = added.at[slot, pl.ds(0, term.shape[0])]
        return pltpu.make_async_copy(term, spot, added_sems.at[slot])

    for step in range(steps):
        each(step, lambda copy: copy.start())
        for slot, (_, wanted, _) in enumerate(adds):
            if wanted == step:
                added_copy(slot).start()

    for step in range(steps):
        each(step, lambda copy: copy.wait())
        for slot, (_, wanted, _) in enumerate(adds):
            if wanted == step:
                added_copy(slot).wait()
        at = 0
        for piece in rows:
            count = piece.shape[0]
            if not any(
                wanted == step and first <= at < first + ref.shape[-2]
                for ref, places in zip(results, outs)
                for wanted, _, first in places
            ):
                at += count
                continue
            value = jnp.dot(piece[...], held[step], preferred_element_type=F32)
            for slot, (_, wanted, first) in enumerate(adds):
                size = terms[slot].shape[-2]
                if wanted == step and first <= at < first + size:
                    value = value + added[slot, at - first : at - first + count].astype(F32)
            for ref, places in zip(results, outs):
                for wanted, lead, first in places:
                    size = ref.shape[-2]
                    if wanted == step and first <= at < first + size:
                        spot = slice(at - first, at - first + count)
                        if lead is None:
                            ref[spot] = value.astype(BF)
                        else:
                            ref[lead, spot] = value.astype(BF)
            at += count


def product(order, items, pieces, terms, shapes, outs):
    rows = sum(piece.shape[0] for piece in items)
    depth, q = pieces[0][0].shape
    steps = order.shape[0]
    flat = [
        pltpu.with_memory_space_constraint(part, pltpu.HBM) for block in pieces for part in block
    ]
    hbm = pl.BlockSpec(memory_space=pltpu.HBM)
    vmem = pl.BlockSpec(memory_space=pltpu.VMEM)
    slots = max(1, len(terms))
    return pl.pallas_call(
        functools.partial(
            product_kernel,
            items=len(items),
            pieces=tuple(len(block) for block in pieces),
            steps=steps,
            adds=tuple(term[1:] for term in terms),
            outs=outs,
        ),
        in_specs=[pl.BlockSpec(memory_space=pltpu.SMEM)]
        + [vmem] * len(items)
        + [hbm] * (len(flat) + len(terms)),
        out_specs=[vmem] * len(shapes),
        out_shape=[jax.ShapeDtypeStruct(shape, BF) for shape in shapes],
        scratch_shapes=[
            pltpu.VMEM((steps, depth, q), BF),
            pltpu.SemaphoreType.DMA((steps, 2)),
            pltpu.VMEM((slots, rows if terms else 16, q), BF),
            pltpu.SemaphoreType.DMA((slots,)),
        ],
        compiler_params=params(SMALL_LIMIT),
        cost_estimate=pl.CostEstimate(
            flops=2 * rows * depth * q * steps,
            bytes_accessed=2 * (rows * depth + steps * (depth * q + rows * q)),
            transcendentals=0,
        ),
        name="product",
    )(order, *items, *flat, *[term[0] for term in terms])


def place_kernel(dests, *refs, sources, count, cap, parts):
    refs = list(refs)
    terms = [[refs.pop(0) for _ in range(n)] for n in parts]
    out, total, used, held, sems = refs
    copies = []
    for at, term in enumerate(terms):
        row = 0
        for part, ref in enumerate(term):
            spot = held.at[at, pl.ds(row, ref.shape[0])]
            copies.append(pltpu.make_async_copy(ref, spot, sems.at[at, part]))
            row += ref.shape[0]
    for copy in copies:
        copy.start()
    out[...] = jnp.zeros_like(out)
    for copy in copies:
        copy.wait()
    value = held[0].astype(F32)
    for at in range(1, len(parts)):
        value = value + held[at].astype(F32)
    total[...] = value
    peers = out.shape[0]
    rows = out.shape[2]
    for s in range(sources):

        @pl.loop(0, peers, unroll=8)
        def _(d):
            used[d] = 0

        @pl.loop(0, count, unroll=32)
        def _(j, s=s):
            d = dests[s * count + j]
            rank = used[d]
            used[d] = rank + 1
            start = pl.multiple_of((s * count + j) * rows, rows)
            out[d, s * cap + rank] = total[pl.ds(start, rows), :].astype(BF)


def place(dests, terms, peers, sources, count, cap, rows):
    flat = [part for term in terms for part in term]
    q = flat[0].shape[1]
    shape = (peers, sources * cap, rows, q)
    size = sources * count * rows
    return pl.pallas_call(
        functools.partial(
            place_kernel,
            sources=sources,
            count=count,
            cap=cap,
            parts=tuple(len(term) for term in terms),
        ),
        grid_spec=pltpu.PrefetchScalarGridSpec(
            num_scalar_prefetch=1,
            grid=(1,),
            in_specs=[pl.BlockSpec(memory_space=pltpu.HBM)] * len(flat),
            out_specs=pl.BlockSpec(shape, lambda s, o: (0, 0, 0, 0)),
            scratch_shapes=[
                pltpu.VMEM((size, q), F32),
                pltpu.SMEM((peers,), jnp.int32),
                pltpu.VMEM((len(terms), size, q), BF),
                pltpu.SemaphoreType.DMA((len(terms), 2)),
            ],
        ),
        out_shape=jax.ShapeDtypeStruct(shape, BF),
        compiler_params=params(SMALL_LIMIT),
        cost_estimate=pl.CostEstimate(
            flops=4 * size * q, bytes_accessed=10 * size * q, transcendentals=0
        ),
        name="place",
    )(dests, *flat)


def final_kernel(part, out, *, offsets, nx, cap):
    q = part.shape[3]
    for z in range(part.shape[0] // nx):
        for at, d in enumerate(offsets):
            for x in range(nx):
                slot = (z * nx + (x - d) % nx) * cap
                out[slot : slot + cap, :, x * q : (x + 1) * q] = part[
                    z * nx + x, at * cap : (at + 1) * cap
                ]


def finish(arrived, offsets, nx, cap):
    peers, slots, rows, q = arrived.shape
    steps = 2
    return pl.pallas_call(
        functools.partial(final_kernel, offsets=offsets, nx=nx, cap=cap),
        grid=(steps,),
        in_specs=[pl.BlockSpec((peers // steps, slots, rows, q), lambda s: (s, 0, 0, 0))],
        out_specs=pl.BlockSpec((peers * cap // steps, rows, nx * q), lambda s: (s, 0, 0)),
        out_shape=jax.ShapeDtypeStruct((peers * cap, rows, nx * q), BF),
        compiler_params=params(SMALL_LIMIT),
        name="finish",
    )(arrived)


def per_device(integrals, occupied_coeffs, metric, mu_block, pair_count, destination):
    nz, nx, ny = lax.axis_size("z"), lax.axis_size("x"), lax.axis_size("y")
    peers = nz * nx
    count = destination.shape[0]
    cap = max(2, (2 * count + peers - 1) // peers)
    _, mu_width, nu, p_local = integrals.shape
    orbitals, local_width = occupied_coeffs.shape
    item_rows = nu * orbitals // count

    def hop(value, axis, size, step):
        return lax.ppermute(value, axis, shift(size, step))

    mid = metric.shape[0] // 2
    up, down = [metric], [metric]
    for _ in range(nz // 2 - 1):
        up.append(hop(up[-1], "z", nz, 1))
        down.append(hop(down[-1], "z", nz, -1))
    far = (hop(up[-1][:mid], "z", nz, 1), hop(down[-1][mid:], "z", nz, -1))
    pieces = [(block,) for block in up] + [far] + [(block,) for block in down[:0:-1]]

    dest_row = jnp.pad(destination.astype(BF)[None], ((0, 8 - orbitals - 1), (0, local_width - count)))
    packed = jnp.concatenate([occupied_coeffs, dest_row], axis=0)
    packed = lax.all_to_all(
        jnp.broadcast_to(packed[None], (peers,) + packed.shape), ("z", "x"), 0, 0, tiled=True
    )
    blocks_per = local_width // mu_width
    where = jnp.stack([mu_block[0] // blocks_per, mu_block[0] % blocks_per, pair_count[0]])
    halves = half_transform(where, packed, integrals[0], orbitals)

    half = halves.shape[0] // 2
    ahead = hop(halves, "x", nx, 1)
    behind = hop(halves, "x", nx, -1)
    far_low = hop(ahead[:half], "x", nx, 1)
    far_high = hop(behind[half:], "x", nx, -1)
    items = (halves, ahead, behind, far_low, far_high)
    offsets = (0, 1, 3, 2)

    z, x, y, core = (lax.axis_index(name) for name in ("z", "x", "y", "core"))
    dests = packed[:, orbitals, :count].astype(jnp.int32)
    rows_of = jnp.concatenate(
        [lax.dynamic_index_in_dim(dests, z * nx + (x - d) % nx, 0, False) for d in offsets]
    )
    def order_of(turn, owner_core):
        return jnp.stack([(z - 2 * ((y + k) % ny) - owner_core) % nz for k in turn]).astype(jnp.int32)

    rows, q = halves.shape[0] * nx, metric.shape[1]
    near = rows // 2
    swap = [(0, 1), (1, 0)]
    first, second = product(
        order_of((2, 0, 1, 3), 1 - core),
        items,
        pieces,
        (),
        ((2, rows, q), (2, rows, q)),
        (((0, 0, 0), (1, 1, 0)), ((2, 0, 0), (3, 1, 0))),
    )
    first = lax.ppermute(first, "core", swap)
    second = lax.ppermute(second, "core", swap)
    low, high = product(
        order_of((2,), core),
        items,
        pieces,
        ((first, 0, 0, 0),),
        ((near, q), (near, q)),
        (((0, None, 0),), ((0, None, near),)),
    )
    made = low
    low, high = hop(low, "y", ny, -1), hop(high, "y", ny, 1)
    right_low, left_high = product(
        lax.optimization_barrier((order_of((1, 3), core), made))[0],
        items,
        pieces,
        ((second, 0, 0, 0), (second, 1, 1, 0)),
        ((near, q), (near, q)),
        (((0, None, 0),), ((1, None, near),)),
    )
    right_high, left_low = product(
        order_of((1, 3), core),
        items,
        pieces,
        ((second, 0, 0, 0), (second, 1, 1, 0), (high, None, 0, near), (low, None, 1, 0)),
        ((near, q), (near, q)),
        (((0, None, near),), ((1, None, 0),)),
    )
    (kept,) = product(
        order_of((0,), core),
        items,
        pieces,
        ((first, 1, 0, 0),),
        ((rows, q),),
        (((0, None, 0),),),
    )
    terms = [
        (kept,),
        (hop(right_low, "y", ny, 1), hop(right_high, "y", ny, 1)),
        (hop(left_low, "y", ny, -1), hop(left_high, "y", ny, -1)),
    ]
    outgoing = place(
        rows_of, terms, peers, len(offsets), count, cap, item_rows
    )
    arrived = lax.all_to_all(outgoing, ("z", "x"), 0, 0, tiled=True)
    return finish(arrived, offsets, nx, cap)


def solution(mesh):
    grid = mesh.devices.reshape(8, 4, mesh.shape["narrow"] // 2, 2)
    fine = Mesh(grid, ("z", "x", "y", "core"))
    wide, narrow = ("z", "x"), ("y", "core")
    placed = (
        P(wide, None, None, narrow),
        P(None, wide),
        P(narrow, wide),
        P(wide),
        P(wide),
        P(wide),
    )
    return jax.shard_map(
        per_device, mesh=fine, in_specs=placed, out_specs=P(wide, None, narrow), check_vma=False
    )
```
